32 devices in a mesh: seq: 8 (over y, x, core), tensor: 4 (over z).
Axes of the slice: x: 2, y: 2, z: 4, core: 2. Of those that a mesh axis runs over, the one named last changes fastest.
Arguments:
- hidden: bfloat16 [8192, 3072], P('seq', 'tensor'), may hold values from -6 to 6
- norm_gain: float32 [3072], replicated, may hold values from 0.1 to 1.9
- query_weight: bfloat16 [3072, 4096], P(None, 'tensor'), may hold values from -0.25 to 0.25
- key_weight: bfloat16 [3072, 4096], P(None, 'tensor'), may hold values from -2 to 2
- value_weight: bfloat16 [3072, 4096], P(None, 'tensor'), may hold values from -0.109375 to 0.109375
- output_weight: bfloat16 [4096, 3072], P('tensor'), may hold values from -1.25 to 1.25
- final_gain: float32 [3072], replicated, may hold values from 0.1 to 1.9
- reward_weight: float32 [3072], replicated, may hold values from -6 to 6
- token_ids: int32 [8192], P(('seq', 'tensor')), may hold values from 0 to 255999, as said below
- index_samples: float32 [8, 8, 8192], P(None, None, ('seq', 'tensor')), may hold values from -6 to 6
- feat_weight: float32 [3072, 256], replicated, may hold values from -0.109375 to 0.109375
- index_weight: float32 [8, 256], replicated, may hold values from -2 to 2
- first_bias: float32 [256], replicated, may hold values from -3 to 3
- middle_weight: float32 [256, 256], replicated, may hold values from -0.375 to 0.375
- second_bias: float32 [256], replicated, may hold values from -3 to 3
- head_weight: float32 [256, 8], replicated, may hold values from -0.375 to 0.375
- pair_ids: int32 [8, 2], replicated, may hold values from 0 to 15, all different within a row
Outputs:
- features: bfloat16 [8192, 3072], P(('seq', 'tensor'))
- pair_margin: float32 [8, 8], replicated
- grad_feature: float32 [3072, 256], P(('seq', 'tensor'))
- grad_index: float32 [8, 256], replicated
- grad_first: float32 [256], replicated
- grad_middle: float32 [256, 256], replicated
- grad_second: float32 [256], replicated
- grad_head: float32 [256, 8], replicated
The draws below stay inside these ranges and needn't reach their ends.
Inputs may be any that keep to these rules, and one draw needn't show every extreme that they name: `token_ids`: in each response of 512 positions the positions before its last valid one hold ids from 2 to 255999, the last valid one holds 1 and the positions after it hold 0; every response has at least 128 valid tokens and at least one 0; the first position of the first response holds 255999. `pair_ids`: each row names two different responses, chosen first; every response stands in exactly one pair.
All inputs are finite; a program needn't handle non-finite values.
Results may differ from the reference program's by a relative error of at most 0.012.
The reference program's roundings to bfloat16 on the way count: a program that leaves them out, or rounds other values in their place, can miss the bound.
Values may be sent and summed in bfloat16 or wider, within the bound.
A program may use at most 128 MiB of HBM per device.

```python
import jax
import jax.numpy as jnp
from jax import lax

D = 3072
HEADS = 16
HEAD_DIM = 256
VOCAB = 256000
EPI = 256
INDEX_DIM = 8
SAMPLES = 8
RESP_LEN = 512
RESPONSES = 16
PAIRS = 8
TOKENS = 8192


def paired_weights(key):
    query_key = jax.random.fold_in(key, 101)
    noise_key = jax.random.fold_in(key, 202)
    matrix_shape = (D, HEADS * HEAD_DIM)
    spread_factor = 0.5 * D ** (-0.5)
    query_part = jnp.clip(jax.random.normal(query_key, matrix_shape, jnp.float32), -5.0, 5.0) * spread_factor
    noise_part = jnp.clip(jax.random.normal(noise_key, matrix_shape, jnp.float32), -5.0, 5.0) * spread_factor
    key_part = noise_part
    return (query_part, key_part)


def draw_query_weight(key, part):
    return paired_weights(key)[0].astype(jnp.bfloat16)


def draw_key_weight(key, part):
    return paired_weights(key)[1].astype(jnp.bfloat16)


def draw_token_ids(key, part):
    length_key = jax.random.fold_in(key, 11)
    word_key = jax.random.fold_in(key, 12)
    lengths = jax.random.randint(length_key, (RESPONSES,), RESP_LEN // 4, RESP_LEN, dtype=jnp.int32)
    positions = jnp.arange(RESP_LEN, dtype=jnp.int32)[None, :]
    rows = jnp.arange(RESPONSES, dtype=jnp.int32)[:, None]
    words = jax.random.randint(word_key, (RESPONSES, RESP_LEN), 2, VOCAB, dtype=jnp.int32)
    words = jnp.where((rows == 0) & (positions == 0), VOCAB - 1, words)
    last_valid = lengths[:, None] - 1
    table = jnp.where(positions < last_valid, words, jnp.where(positions == last_valid, 1, 0))
    return table.reshape(TOKENS).astype(jnp.int32)


def steps_of(stream_key, shape, cuts, low, high):
    level = 1.0
    for position, blocks in cuts:
        heights = jax.random.uniform(jax.random.fold_in(jax.random.fold_in(stream_key, 6), position), (blocks,), jnp.float32, low / len(cuts), high / len(cuts))
        level = level * jnp.repeat(jnp.exp(heights), shape[position] // blocks).reshape((-1,) + (1,) * (len(shape) - 1 - position))
    return level


def picks_of(stream_key, rows, count, top, lift):
    ranking = jax.random.permutation(jax.random.fold_in(stream_key, 1), count)
    favour = ranking
    for power in range(3):
        favour = favour * favour // count
    favour = favour * lift // count
    chance = jax.random.randint(jax.random.fold_in(stream_key, 2), (rows, count), 0, 4096) + favour
    holders = jax.random.permutation(jax.random.fold_in(stream_key, 3), rows)[jnp.arange(count) % rows]
    chance = jnp.where(jnp.arange(rows)[:, None] == holders[None, :], 1 << 14, chance)
    priority = chance * count + jnp.arange(count)
    return lax.top_k(priority.astype(jnp.int32), top)[1].astype(jnp.int32)


def noise(own_key, extent, spread, limit, shards=(), kind=jnp.bfloat16):
    level = steps_of(own_key, extent, shards, -0.22, 0.18) if shards else 1.0
    drawn = jax.random.normal(own_key, extent, jnp.float32) * spread * level
    return jnp.minimum(jnp.maximum(drawn, -limit), limit).astype(kind)


def setup_inputs(seed: int = 0) -> dict:
    streams_of = jax.random.split(jax.random.key(seed), 18)
    return {
        "hidden": noise(streams_of[0], (TOKENS, D), 1.0, 6.0, ((0, 8), (1, 4))),
        "norm_gain": jnp.clip(1.0 + 0.18 * jax.random.normal(streams_of[1], (D,), jnp.float32), 0.1, 1.9),
        "query_weight": draw_query_weight(jax.random.fold_in(streams_of[17], 71), 0),
        "key_weight": draw_key_weight(jax.random.fold_in(streams_of[17], 71), 0),
        "value_weight": noise(streams_of[4], (D, HEADS * HEAD_DIM), D ** -0.5, 0.109375, ((1, 4),)),
        "output_weight": noise(streams_of[5], (HEADS * HEAD_DIM, D), 0.08, 1.25, ((0, 4),)),
        "final_gain": jnp.clip(1.0 + 0.18 * jax.random.normal(streams_of[6], (D,), jnp.float32), 0.1, 1.9),
        "reward_weight": noise(streams_of[7], (D,), 0.5, 6.0, (), jnp.float32),
        "token_ids": draw_token_ids(jax.random.fold_in(streams_of[17], 71), 0),
        "index_samples": noise(streams_of[9], (SAMPLES, INDEX_DIM, TOKENS), 1.0, 6.0, ((2, 32),), jnp.float32),
        "feat_weight": noise(streams_of[10], (D, EPI), D ** -0.5, 0.109375, (), jnp.float32),
        "index_weight": noise(streams_of[11], (INDEX_DIM, EPI), INDEX_DIM ** -0.5, 2.0, (), jnp.float32),
        "first_bias": noise(streams_of[12], (EPI,), 0.5, 3.0, (), jnp.float32),
        "middle_weight": noise(streams_of[13], (EPI, EPI), EPI ** -0.5, 0.375, (), jnp.float32),
        "second_bias": noise(streams_of[14], (EPI,), 0.5, 3.0, (), jnp.float32),
        "head_weight": noise(streams_of[15], (EPI, INDEX_DIM), EPI ** -0.5, 0.375, (), jnp.float32),
        "pair_ids": picks_of(streams_of[16], PAIRS, RESPONSES, 2, 0),
    }


norm_eps = 1e-06
rope_base = 10000.0
gelu_coef = 0.044715
gelu_root = 0.7978845608028654
masked_score = -1e+30

def rms_scale(rows, gain):
    mean_square = lax.optimization_barrier(jnp.mean(rows * rows, axis=-1, keepdims=True))
    return rows * lax.rsqrt(mean_square + norm_eps) * (1.0 + gain)

def rotate_pairs(entries, positions):
    half_dim = entries.shape[-1] // 2
    freqs = rope_base ** (-(jnp.arange(half_dim, dtype=jnp.float32) * 2.0) / entries.shape[-1])
    angles = positions.astype(jnp.float32)[:, None] * freqs[None, :]
    cosine = jnp.cos(angles)[:, None, :]
    sine = jnp.sin(angles)[:, None, :]
    first_half = entries[..., :half_dim]
    second_half = entries[..., half_dim:]
    return jnp.concatenate([first_half * cosine - second_half * sine, second_half * cosine + first_half * sine], axis=-1)

def gelu_tanh(inputs):
    return 0.5 * inputs * (1.0 + jnp.tanh(gelu_root * (inputs + gelu_coef * inputs * inputs * inputs)))

def epinet_rewards(params, feat32, samples):
    feat_weight, index_weight, first_bias, middle_weight, second_bias, head_weight = params
    feat_part = jnp.dot(feat32, feat_weight, precision=lax.Precision.HIGHEST)
    index_part = jnp.einsum('sit,ie->ste', samples, index_weight, precision=lax.Precision.HIGHEST)
    first_act = gelu_tanh(feat_part[None, :, :] + index_part + first_bias)
    second_pre = jnp.einsum('ste,ef->stf', first_act, middle_weight, precision=lax.Precision.HIGHEST) + second_bias
    second_act = gelu_tanh(second_pre)
    head_out = jnp.einsum('ste,ei->sti', second_act, head_weight, precision=lax.Precision.HIGHEST)
    return jnp.einsum('sti,sit->st', head_out, samples, precision=lax.Precision.HIGHEST)

def reference(hidden, norm_gain, query_weight, key_weight, value_weight, output_weight, final_gain, reward_weight, token_ids, index_samples, feat_weight, index_weight, first_bias, middle_weight, second_bias, head_weight, pair_ids):
    normed = rms_scale(hidden.astype(jnp.float32), norm_gain).astype(jnp.bfloat16)
    blocks = normed.reshape(RESPONSES, RESP_LEN, D)
    positions = jnp.arange(RESP_LEN, dtype=jnp.int32)
    causal = positions[None, :] <= positions[:, None]

    def one_response(block):
        queries = jnp.dot(block, query_weight, preferred_element_type=jnp.float32).reshape(RESP_LEN, HEADS, HEAD_DIM)
        queries = rotate_pairs(queries, positions).astype(jnp.bfloat16)
        key_rows = jnp.dot(block, key_weight, preferred_element_type=jnp.float32).reshape(RESP_LEN, HEADS, HEAD_DIM)
        key_rows = rotate_pairs(key_rows, positions).astype(jnp.bfloat16)
        value_rows = jnp.dot(block, value_weight, preferred_element_type=jnp.float32).astype(jnp.bfloat16).reshape(RESP_LEN, HEADS, HEAD_DIM)
        scores = jnp.einsum('qhd,khd->hqk', queries.astype(jnp.float32), key_rows.astype(jnp.float32)) * HEAD_DIM ** (-0.5)
        scores = jnp.where(causal[None, :, :], scores, masked_score)
        highest = lax.optimization_barrier(jnp.max(scores, axis=-1, keepdims=True))
        weights = jnp.exp(scores - highest)
        probs = (weights / lax.optimization_barrier(jnp.sum(weights, axis=-1, keepdims=True))).astype(jnp.bfloat16)
        attended = jnp.einsum('hqk,khd->qhd', probs.astype(jnp.float32), value_rows.astype(jnp.float32)).astype(jnp.bfloat16)
        attended = attended.reshape(RESP_LEN, HEADS * HEAD_DIM)
        return jnp.dot(attended, output_weight, preferred_element_type=jnp.float32)
    mixed = lax.map(one_response, blocks).reshape(TOKENS, D)
    features = rms_scale(hidden.astype(jnp.float32) + mixed, final_gain).astype(jnp.bfloat16)
    feat32 = features.astype(jnp.float32)
    base = jnp.dot(feat32, reward_weight, precision=lax.Precision.HIGHEST)
    valid = (token_ids != 0).astype(jnp.float32)
    counts = lax.optimization_barrier(jnp.sum(valid.reshape(RESPONSES, RESP_LEN), axis=1))

    def loss_of(params):
        epi = epinet_rewards(params, feat32, index_samples)
        rewards = (base[None, :] + epi) * valid[None, :]
        totals = lax.optimization_barrier(jnp.sum(rewards.reshape(SAMPLES, RESPONSES, RESP_LEN), axis=2))
        means = totals / counts[None, :]
        margin = (means[:, pair_ids[:, 0]] - means[:, pair_ids[:, 1]]).T
        return (jnp.sum(jax.nn.softplus(-margin)), margin)
    params = (feat_weight, index_weight, first_bias, middle_weight, second_bias, head_weight)
    loss, pullback, margin = jax.vjp(loss_of, params, has_aux=True)
    grads = pullback(jnp.ones((), jnp.float32))[0]
    return (features, margin, grads[0], grads[1], grads[2], grads[3], grads[4], grads[5])
```

```python
import functools

import jax
import jax.numpy as jnp
from jax import lax
from jax.experimental import pallas as pl
from jax.experimental.pallas import tpu as pltpu
from jax.sharding import PartitionSpec as P

HEAD_DIM = 256
RESP_LEN = 512
MESH = pl.DeviceIdType.MESH

norm_eps = 1e-06
rope_base = 10000.0
gelu_coef = 0.044715
gelu_root = 0.7978845608028654
masked_score = -1e30


def gelu_tanh(inputs):
    return (
        0.5 * inputs * (1.0 + jnp.tanh(gelu_root * (inputs + gelu_coef * inputs * inputs * inputs)))
    )


def gelu_slope(inputs):
    tangent = jnp.tanh(gelu_root * (inputs + gelu_coef * inputs * inputs * inputs))
    inner_slope = gelu_root * (1.0 + 3.0 * gelu_coef * inputs * inputs)
    return 0.5 * (1.0 + tangent) + 0.5 * inputs * (1.0 - tangent * tangent) * inner_slope


def attention_kernel(
    x_ref, gain_ref, wq_ref, wk_ref, wv_ref, cos_ref, sin_ref, out_ref, normed_ref
):
    parts, rows, width = x_ref.shape
    step = 64

    @pl.when(pl.program_id(0) == 0)
    def _():
        def body(i, carry):
            at = pl.ds(pl.multiple_of(i * step, step), step)
            total = jnp.zeros((step, 1), jnp.float32)
            for p in range(parts):
                x = x_ref[p, at, :].astype(jnp.float32)
                total = total + jnp.sum(x * x, axis=-1, keepdims=True)
            scale = lax.rsqrt(total / (parts * width) + norm_eps)
            for p in range(parts):
                x = x_ref[p, at, :].astype(jnp.float32)
                gain = 1.0 + gain_ref[p : p + 1, :]
                normed_ref[at, p * width : (p + 1) * width] = (x * scale * gain).astype(
                    jnp.bfloat16
                )
            return carry

        lax.fori_loop(0, rows // step, body, 0)

    normed = normed_ref[...]
    cosine = cos_ref[...]
    sine = sin_ref[...]
    half = HEAD_DIM // 2

    def rotated(w_ref):
        full = jnp.dot(normed, w_ref[...], preferred_element_type=jnp.float32)
        a = full[:, :half]
        b = full[:, half:]
        return jnp.concatenate([a * cosine - b * sine, b * cosine + a * sine], axis=-1).astype(
            jnp.bfloat16
        )

    queries = rotated(wq_ref)
    keys = rotated(wk_ref)
    values = jnp.dot(normed, wv_ref[...], preferred_element_type=jnp.float32).astype(jnp.bfloat16)
    scores = lax.dot_general(
        queries, keys, (((1,), (1,)), ((), ())), preferred_element_type=jnp.float32
    ) * HEAD_DIM ** (-0.5)
    q_pos = lax.broadcasted_iota(jnp.int32, scores.shape, 0)
    k_pos = lax.broadcasted_iota(jnp.int32, scores.shape, 1)
    scores = jnp.where(k_pos <= q_pos, scores, masked_score)
    highest = jnp.max(scores, axis=-1, keepdims=True)
    weights = jnp.exp(scores - highest)
    probs = (weights / jnp.sum(weights, axis=-1, keepdims=True)).astype(jnp.bfloat16)
    out_ref[...] = jnp.dot(probs, values, preferred_element_type=jnp.float32).astype(jnp.bfloat16)


def attend(x, gain, wq, wk, wv, cosine, sine):
    parts, rows, width = x.shape
    depth = parts * width
    heads = wq.shape[1] // HEAD_DIM
    weight = pl.BlockSpec((depth, HEAD_DIM), lambda h: (0, h))
    table = pl.BlockSpec((rows, HEAD_DIM // 2), lambda h: (0, 0))
    return pl.pallas_call(
        attention_kernel,
        grid=(heads,),
        out_shape=jax.ShapeDtypeStruct((rows, heads * HEAD_DIM), jnp.bfloat16),
        in_specs=[
            pl.BlockSpec((parts, rows, width), lambda h: (0, 0, 0)),
            pl.BlockSpec((parts, width), lambda h: (0, 0)),
            weight,
            weight,
            weight,
            table,
            table,
        ],
        out_specs=pl.BlockSpec((rows, HEAD_DIM), lambda h: (0, h)),
        scratch_shapes=[pltpu.VMEM((rows, depth), jnp.bfloat16)],
        compiler_params=pltpu.CompilerParams(vmem_limit_bytes=48 * 1024 * 1024),
        cost_estimate=pl.CostEstimate(
            flops=2 * rows * depth * HEAD_DIM * heads * 3 + 4 * rows * rows * HEAD_DIM * heads,
            bytes_accessed=rows * depth * 2 + 3 * depth * HEAD_DIM * heads * 2,
            transcendentals=rows * rows * heads,
        ),
    )(x, gain, wq, wk, wv, cosine, sine)


def push(axis, count, sources, targets, send_sems, recv_sems):
    me = lax.axis_index(axis)
    copies = []
    for k in range(1, count):
        peer = lax.rem(me + k, count)
        for j, (source, target) in enumerate(zip(sources, targets)):
            copy = pltpu.make_async_remote_copy(
                src_ref=source(peer),
                dst_ref=target.at[k],
                send_sem=send_sems.at[j, k],
                recv_sem=recv_sems.at[j, k],
                device_id={axis: peer},
                device_id_type=MESH,
            )
            copy.start()
            copies.append(copy)
    return copies


def greet(seq_count, tp_count):
    barrier = pltpu.get_barrier_semaphore()
    for axis, count in (("seq", seq_count), ("tensor", tp_count)):
        me = lax.axis_index(axis)
        for k in range(1, count):
            pl.semaphore_signal(
                barrier, inc=1, device_id={axis: lax.rem(me + k, count)}, device_id_type=MESH
            )
    pl.semaphore_wait(barrier, seq_count + tp_count - 2)


def ordered_sum(axis, count, slots):
    me = lax.axis_index(axis)
    total = slots[lax.rem(me + count, count)]
    for origin in range(1, count):
        total = total + slots[lax.rem(me - origin + count, count)]
    return total


def totals_kernel(
    seq_count, tp_count, part_ref, out_ref, first, mid, second, send1, recv1, send2, recv2
):
    greet(seq_count, tp_count)
    copies = push("seq", seq_count, [lambda p: part_ref], [first], send1, recv1)
    first[0] = part_ref[...]
    for copy in copies:
        copy.wait()
    mid[...] = ordered_sum("seq", seq_count, first)
    copies = push("tensor", tp_count, [lambda p: mid], [second], send2, recv2)
    second[0] = mid[...]
    for copy in copies:
        copy.wait()
    out_ref[...] = ordered_sum("tensor", tp_count, second)


def sum_everywhere(part, seq_count, tp_count):
    rows, lanes = part.shape
    vmem = pl.BlockSpec(memory_space=pltpu.VMEM)
    return pl.pallas_call(
        functools.partial(totals_kernel, seq_count, tp_count),
        out_shape=jax.ShapeDtypeStruct(part.shape, jnp.float32),
        in_specs=[vmem],
        out_specs=vmem,
        scratch_shapes=[
            pltpu.VMEM((seq_count, rows, lanes), jnp.float32),
            pltpu.VMEM((rows, lanes), jnp.float32),
            pltpu.VMEM((tp_count, rows, lanes), jnp.float32),
            pltpu.SemaphoreType.DMA((1, seq_count)),
            pltpu.SemaphoreType.DMA((1, seq_count)),
            pltpu.SemaphoreType.DMA((1, tp_count)),
            pltpu.SemaphoreType.DMA((1, tp_count)),
        ],
        compiler_params=pltpu.CompilerParams(collective_id=1, has_side_effects=True),
    )(part)


def grads_kernel(
    seq_count,
    tp_count,
    feat_ref,
    small_ref,
    feat_out,
    small_out,
    feat1,
    small1,
    feat_mid,
    small_mid,
    feat2,
    small2,
    small3,
    send1,
    recv1,
    send2,
    recv2,
    send3,
    recv3,
):
    seq_me = lax.axis_index("seq")
    tp_me = lax.axis_index("tensor")
    greet(seq_count, tp_count)
    sources = [lambda p: feat_ref.at[p], lambda p: small_ref.at[p]]
    copies = push("seq", seq_count, sources, [feat1, small1], send1, recv1)
    small1[0] = small_ref[seq_me]
    for copy in copies:
        copy.wait()
    small_mid[...] = ordered_sum("seq", seq_count, small1)

    def body(i, carry):
        total = feat_ref[seq_me, i].astype(jnp.float32)
        for k in range(1, seq_count):
            total = total + feat1[k, i].astype(jnp.float32)
        feat_mid[i] = total
        return carry

    lax.fori_loop(0, tp_count, body, 0)
    sources = [lambda p: feat_mid.at[p], lambda p: small_mid]
    copies = push("tensor", tp_count, sources, [feat2, small2], send2, recv2)
    small2[0] = small_mid[...]
    for copy in copies:
        copy.wait()
    total = feat_mid[tp_me]
    for k in range(1, tp_count):
        total = total + feat2[k]
    feat_out[...] = total
    small3[0] = ordered_sum("tensor", tp_count, small2)
    copies = push("seq", seq_count, [lambda p: small3.at[0]], [small3], send3, recv3)
    for copy in copies:
        copy.wait()
    for origin in range(seq_count):
        small_out[origin] = small3[lax.rem(seq_me - origin + seq_count, seq_count)]


def reduce_grads(feat, small, seq_count, tp_count):
    rows, width = feat.shape[2:]
    extra = small.shape[1]
    vmem = pl.BlockSpec(memory_space=pltpu.VMEM)
    dma = pltpu.SemaphoreType.DMA
    f32 = jnp.float32
    return pl.pallas_call(
        functools.partial(grads_kernel, seq_count, tp_count),
        out_shape=(
            jax.ShapeDtypeStruct((rows, width), f32),
            jax.ShapeDtypeStruct((seq_count, extra, width), f32),
        ),
        in_specs=[vmem, vmem],
        out_specs=(vmem, vmem),
        scratch_shapes=[
            pltpu.VMEM((seq_count, tp_count, rows, width), feat.dtype),
            pltpu.VMEM((seq_count, extra, width), f32),
            pltpu.VMEM((tp_count, rows, width), f32),
            pltpu.VMEM((extra, width), f32),
            pltpu.VMEM((tp_count, rows, width), f32),
            pltpu.VMEM((tp_count, extra, width), f32),
            pltpu.VMEM((seq_count, extra, width), f32),
            dma((2, seq_count)),
            dma((2, seq_count)),
            dma((2, tp_count)),
            dma((2, tp_count)),
            dma((1, seq_count)),
            dma((1, seq_count)),
        ],
        compiler_params=pltpu.CompilerParams(
            collective_id=2, has_side_effects=True, vmem_limit_bytes=32 * 1024 * 1024
        ),
    )(feat, small)


def shards(
    hidden,
    norm_gain,
    query_weight,
    key_weight,
    value_weight,
    output_weight,
    final_gain,
    reward_weight,
    token_ids,
    index_samples,
    feat_weight,
    index_weight,
    first_bias,
    middle_weight,
    second_bias,
    head_weight,
    pair_ids,
):
    highest = lax.Precision.HIGHEST
    tp_count = lax.axis_size("tensor")
    seq_count = lax.axis_size("seq")
    tp_index = lax.axis_index("tensor")
    seq_index = lax.axis_index("seq")
    tok_seq, part_width = hidden.shape
    width = part_width * tp_count
    local_resp = tok_seq // RESP_LEN
    tok_epi = tok_seq // tp_count

    half_dim = HEAD_DIM // 2
    positions = jnp.arange(RESP_LEN, dtype=jnp.int32)
    freqs = rope_base ** (-(jnp.arange(half_dim, dtype=jnp.float32) * 2.0) / HEAD_DIM)
    angles = positions.astype(jnp.float32)[:, None] * freqs[None, :]
    cosine = jnp.cos(angles)
    sine = jnp.sin(angles)

    gain_parts = norm_gain.reshape(tp_count, part_width)
    partials = []
    first_row = tp_index * tok_epi
    own_row = lax.rem(first_row, RESP_LEN)
    own_resp = first_row // RESP_LEN
    own = None
    for r in range(local_resp):
        x = lax.all_gather(hidden[r * RESP_LEN : (r + 1) * RESP_LEN], "tensor", axis=0)
        attended = attend(
            x, gain_parts, query_weight, key_weight, value_weight, cosine, sine
        )
        partials.append(
            jnp.dot(attended, output_weight, preferred_element_type=jnp.float32).astype(
                jnp.bfloat16
            )
        )
        rows = lax.dynamic_slice_in_dim(x, own_row, tok_epi, 1)
        own = rows if own is None else jnp.where(own_resp == r, rows, own)
    residual = jnp.swapaxes(own, 0, 1).reshape(tok_epi, width).astype(jnp.float32)
    partial_out = jnp.concatenate(partials, axis=0)
    mixed = lax.psum_scatter(partial_out, "tensor", scatter_dimension=0, tiled=True)
    summed = residual + mixed.astype(jnp.float32)
    mean_square = jnp.mean(summed * summed, axis=-1, keepdims=True)
    features = (summed * lax.rsqrt(mean_square + norm_eps) * (1.0 + final_gain)).astype(
        jnp.bfloat16
    )

    feat32 = features.astype(jnp.float32)
    base = jnp.dot(feat32, reward_weight, precision=highest)
    feat_part = jnp.dot(feat32, feat_weight, precision=highest)
    index_part = jnp.einsum("sit,ie->ste", index_samples, index_weight, precision=highest)
    first_pre = feat_part[None, :, :] + index_part + first_bias
    first_act = gelu_tanh(first_pre)
    second_pre = (
        jnp.einsum("ste,ef->stf", first_act, middle_weight, precision=highest) + second_bias
    )
    second_act = gelu_tanh(second_pre)
    head_out = jnp.einsum("ste,ei->sti", second_act, head_weight, precision=highest)
    epinet_out = jnp.einsum("sti,sit->st", head_out, index_samples, precision=highest)
    resp_total = 2 * pair_ids.shape[0]
    sample_count = index_samples.shape[0]
    owner = (seq_index * tok_seq + first_row) // RESP_LEN
    slot_ids = jnp.arange(resp_total, dtype=jnp.int32)
    owner_row = (owner == slot_ids).astype(jnp.float32)
    valid = (token_ids != 0).astype(jnp.float32)
    own_total = jnp.sum((base[None, :] + epinet_out) * valid[None, :], axis=1)
    own_count = jnp.sum(valid)
    part = jnp.concatenate([own_total, jnp.full((8,), 0.0, jnp.float32) + own_count])
    part = part[:, None] * owner_row[None, :]
    part = jnp.pad(part, ((0, 0), (0, 128 - resp_total)))
    sums = sum_everywhere(part, seq_count, tp_count)
    totals = sums[:sample_count, :resp_total]
    counts = sums[sample_count, :resp_total]
    means = totals / counts[None, :]
    sign_table = (pair_ids[:, 0:1] == slot_ids[None, :]).astype(jnp.float32) - (
        pair_ids[:, 1:2] == slot_ids[None, :]
    ).astype(jnp.float32)
    margin = jnp.dot(means, sign_table.T, precision=highest)
    pair_margin = margin.T
    margin_grad = -jax.nn.sigmoid(-margin)
    mean_grad = jnp.dot(margin_grad, sign_table, precision=highest) / counts[None, :]
    own_grad = jnp.sum(mean_grad * owner_row[None, :], axis=1)
    reward_grad = own_grad[:, None] * valid[None, :]
    out_grad = jnp.einsum("st,sit->sti", reward_grad, index_samples)
    grad_head = jnp.einsum("ste,sti->ie", second_act, out_grad, precision=highest)
    second_grad = jnp.einsum(
        "sti,ei->ste", out_grad, head_weight, precision=highest
    ) * gelu_slope(second_pre)
    grad_second = jnp.sum(second_grad, axis=(0, 1))
    grad_middle = jnp.einsum("ste,stf->ef", first_act, second_grad, precision=highest)
    first_grad = jnp.einsum(
        "stf,ef->ste", second_grad, middle_weight, precision=highest
    ) * gelu_slope(first_pre)
    grad_first = jnp.sum(first_grad, axis=(0, 1))
    grad_index = jnp.einsum("sit,ste->ie", index_samples, first_grad, precision=highest)
    feat_grad = jnp.sum(first_grad, axis=0)
    grad_feature = jnp.einsum("td,te->de", feat32, feat_grad, precision=highest)

    hidden_units = middle_weight.shape[0]
    index_dim = index_weight.shape[0]
    small = jnp.concatenate(
        [grad_middle, grad_index, grad_head, grad_first[None, :], grad_second[None, :]], axis=0
    )
    used = small.shape[0]
    unit = 8 * seq_count
    padded = (used + unit - 1) // unit * unit
    small = jnp.pad(small, ((0, padded - used), (0, 0)))
    small = small.reshape(seq_count, padded // seq_count, hidden_units)
    feat_blocks = grad_feature.astype(jnp.bfloat16).reshape(
        seq_count, tp_count, width // (seq_count * tp_count), hidden_units
    )
    grad_feature, small = reduce_grads(feat_blocks, small, seq_count, tp_count)
    small = small.reshape(padded, hidden_units)
    at = hidden_units
    return (
        features,
        pair_margin,
        grad_feature,
        small[at : at + index_dim],
        small[at + 2 * index_dim],
        small[:at],
        small[at + 2 * index_dim + 1],
        small[at + index_dim : at + 2 * index_dim].T,
    )


def solution(mesh):
    return jax.shard_map(
        shards,
        mesh=mesh,
        in_specs=(
            P("seq", "tensor"),
            P(),
            P(None, "tensor"),
            P(None, "tensor"),
            P(None, "tensor"),
            P("tensor", None),
            P(),
            P(),
            P(("seq", "tensor")),
            P(None, None, ("seq", "tensor")),
            P(),
            P(),
            P(),
            P(),
            P(),
            P(),
            P(),
        ),
        out_specs=(
            P(("seq", "tensor"), None),
            P(),
            P(("seq", "tensor"), None),
            P(),
            P(),
            P(),
            P(),
            P(),
        ),
        check_vma=False,
    )
```

```python
import functools

import jax
import jax.numpy as jnp
from jax import lax
from jax.experimental import pallas as pl
from jax.experimental.pallas import tpu as pltpu
from jax.sharding import PartitionSpec as P

HEAD_DIM = 256
RESP_LEN = 512
MESH = pl.DeviceIdType.MESH

norm_eps = 1e-06
rope_base = 10000.0
gelu_coef = 0.044715
gelu_root = 0.7978845608028654
masked_score = -1e30


def gelu_tanh(inputs):
    return (
        0.5 * inputs * (1.0 + jnp.tanh(gelu_root * (inputs + gelu_coef * inputs * inputs * inputs)))
    )


def gelu_slope(inputs):
    tangent = jnp.tanh(gelu_root * (inputs + gelu_coef * inputs * inputs * inputs))
    inner_slope = gelu_root * (1.0 + 3.0 * gelu_coef * inputs * inputs)
    return 0.5 * (1.0 + tangent) + 0.5 * inputs * (1.0 - tangent * tangent) * inner_slope


def attention_kernel(
    x_ref, gain_ref, wq_ref, wk_ref, wv_ref, cos_ref, sin_ref, out_ref, normed_ref
):
    parts, rows, width = x_ref.shape
    step = 64

    @pl.when(pl.program_id(0) == 0)
    def _():
        def body(i, carry):
            at = pl.ds(pl.multiple_of(i * step, step), step)
            total = jnp.zeros((step, 1), jnp.float32)
            for p in range(parts):
                x = x_ref[p, at, :].astype(jnp.float32)
                total = total + jnp.sum(x * x, axis=-1, keepdims=True)
            scale = lax.rsqrt(total / (parts * width) + norm_eps)
            for p in range(parts):
                x = x_ref[p, at, :].astype(jnp.float32)
                gain = 1.0 + gain_ref[p : p + 1, :]
                normed_ref[at, p * width : (p + 1) * width] = (x * scale * gain).astype(
                    jnp.bfloat16
                )
            return carry

        lax.fori_loop(0, rows // step, body, 0)

    normed = normed_ref[...]
    cosine = cos_ref[...]
    sine = sin_ref[...]
    half = HEAD_DIM // 2

    def rotated(w_ref):
        full = jnp.dot(normed, w_ref[...], preferred_element_type=jnp.float32)
        a = full[:, :half]
        b = full[:, half:]
        return jnp.concatenate([a * cosine - b * sine, b * cosine + a * sine], axis=-1).astype(
            jnp.bfloat16
        )

    queries = rotated(wq_ref)
    keys = rotated(wk_ref)
    values = jnp.dot(normed, wv_ref[...], preferred_element_type=jnp.float32).astype(jnp.bfloat16)
    scores = lax.dot_general(
        queries, keys, (((1,), (1,)), ((), ())), preferred_element_type=jnp.float32
    ) * HEAD_DIM ** (-0.5)
    q_pos = lax.broadcasted_iota(jnp.int32, scores.shape, 0)
    k_pos = lax.broadcasted_iota(jnp.int32, scores.shape, 1)
    scores = jnp.where(k_pos <= q_pos, scores, masked_score)
    highest = jnp.max(scores, axis=-1, keepdims=True)
    weights = jnp.exp(scores - highest)
    probs = (weights / jnp.sum(weights, axis=-1, keepdims=True)).astype(jnp.bfloat16)
    out_ref[...] = jnp.dot(probs, values, preferred_element_type=jnp.float32).astype(jnp.bfloat16)


def attend(x, gain, wq, wk, wv, cosine, sine):
    parts, rows, width = x.shape
    depth = parts * width
    heads = wq.shape[1] // HEAD_DIM
    weight = pl.BlockSpec((depth, HEAD_DIM), lambda h: (0, h))
    table = pl.BlockSpec((rows, HEAD_DIM // 2), lambda h: (0, 0))
    return pl.pallas_call(
        attention_kernel,
        grid=(heads,),
        out_shape=jax.ShapeDtypeStruct((rows, heads * HEAD_DIM), jnp.bfloat16),
        in_specs=[
            pl.BlockSpec((parts, rows, width), lambda h: (0, 0, 0)),
            pl.BlockSpec((parts, width), lambda h: (0, 0)),
            weight,
            weight,
            weight,
            table,
            table,
        ],
        out_specs=pl.BlockSpec((rows, HEAD_DIM), lambda h: (0, h)),
        scratch_shapes=[pltpu.VMEM((rows, depth), jnp.bfloat16)],
        compiler_params=pltpu.CompilerParams(vmem_limit_bytes=48 * 1024 * 1024),
        cost_estimate=pl.CostEstimate(
            flops=2 * rows * depth * HEAD_DIM * heads * 3 + 4 * rows * rows * HEAD_DIM * heads,
            bytes_accessed=rows * depth * 2 + 3 * depth * HEAD_DIM * heads * 2,
            transcendentals=rows * rows * heads,
        ),
    )(x, gain, wq, wk, wv, cosine, sine)


def push(axis, count, sources, targets, send_sems, recv_sems):
    me = lax.axis_index(axis)
    copies = []
    for k in range(1, count):
        peer = lax.rem(me + k, count)
        for j, (source, target) in enumerate(zip(sources, targets)):
            copy = pltpu.make_async_remote_copy(
                src_ref=source(peer),
                dst_ref=target.at[k],
                send_sem=send_sems.at[j, k],
                recv_sem=recv_sems.at[j, k],
                device_id={axis: peer},
                device_id_type=MESH,
            )
            copy.start()
            copies.append(copy)
    return copies


def greet(seq_count, tp_count):
    barrier = pltpu.get_barrier_semaphore()
    for axis, count in (("seq", seq_count), ("tensor", tp_count)):
        me = lax.axis_index(axis)
        for k in range(1, count):
            pl.semaphore_signal(
                barrier, inc=1, device_id={axis: lax.rem(me + k, count)}, device_id_type=MESH
            )
    pl.semaphore_wait(barrier, seq_count + tp_count - 2)


def ordered_sum(axis, count, slots):
    me = lax.axis_index(axis)
    total = slots[lax.rem(me + count, count)]
    for origin in range(1, count):
        total = total + slots[lax.rem(me - origin + count, count)]
    return total


def totals_kernel(
    seq_count, tp_count, part_ref, out_ref, first, mid, second, send1, recv1, send2, recv2
):
    greet(seq_count, tp_count)
    copies = push("seq", seq_count, [lambda p: part_ref], [first], send1, recv1)
    first[0] = part_ref[...]
    for copy in copies:
        copy.wait()
    mid[...] = ordered_sum("seq", seq_count, first)
    copies = push("tensor", tp_count, [lambda p: mid], [second], send2, recv2)
    second[0] = mid[...]
    for copy in copies:
        copy.wait()
    out_ref[...] = ordered_sum("tensor", tp_count, second)


def sum_everywhere(part, seq_count, tp_count):
    rows, lanes = part.shape
    vmem = pl.BlockSpec(memory_space=pltpu.VMEM)
    return pl.pallas_call(
        functools.partial(totals_kernel, seq_count, tp_count),
        out_shape=jax.ShapeDtypeStruct(part.shape, jnp.float32),
        in_specs=[vmem],
        out_specs=vmem,
        scratch_shapes=[
            pltpu.VMEM((seq_count, rows, lanes), jnp.float32),
            pltpu.VMEM((rows, lanes), jnp.float32),
            pltpu.VMEM((tp_count, rows, lanes), jnp.float32),
            pltpu.SemaphoreType.DMA((1, seq_count)),
            pltpu.SemaphoreType.DMA((1, seq_count)),
            pltpu.SemaphoreType.DMA((1, tp_count)),
            pltpu.SemaphoreType.DMA((1, tp_count)),
        ],
        compiler_params=pltpu.CompilerParams(collective_id=1, has_side_effects=True),
    )(part)


def grads_kernel(
    seq_count,
    tp_count,
    feat_ref,
    small_ref,
    feat_out,
    small_out,
    feat1,
    small1,
    feat_mid,
    small_mid,
    feat2,
    small2,
    small3,
    send1,
    recv1,
    send2,
    recv2,
    send3,
    recv3,
):
    seq_me = lax.axis_index("seq")
    tp_me = lax.axis_index("tensor")
    greet(seq_count, tp_count)
    sources = [lambda p: feat_ref.at[p], lambda p: small_ref.at[p]]
    copies = push("seq", seq_count, sources, [feat1, small1], send1, recv1)
    small1[0] = small_ref[seq_me]
    for copy in copies:
        copy.wait()
    small_mid[...] = ordered_sum("seq", seq_count, small1)

    def body(i, carry):
        total = feat_ref[seq_me, i].astype(jnp.float32)
        for k in range(1, seq_count):
            total = total + feat1[k, i].astype(jnp.float32)
        feat_mid[i] = total
        return carry

    lax.fori_loop(0, tp_count, body, 0)
    sources = [lambda p: feat_mid.at[p], lambda p: small_mid]
    copies = push("tensor", tp_count, sources, [feat2, small2], send2, recv2)
    small2[0] = small_mid[...]
    for copy in copies:
        copy.wait()
    total = feat_mid[tp_me]
    for k in range(1, tp_count):
        total = total + feat2[k]
    feat_out[...] = total
    small3[0] = ordered_sum("tensor", tp_count, small2)
    copies = push("seq", seq_count, [lambda p: small3.at[0]], [small3], send3, recv3)
    for copy in copies:
        copy.wait()
    for origin in range(seq_count):
        small_out[origin] = small3[lax.rem(seq_me - origin + seq_count, seq_count)]


def reduce_grads(feat, small, seq_count, tp_count):
    rows, width = feat.shape[2:]
    extra = small.shape[1]
    vmem = pl.BlockSpec(memory_space=pltpu.VMEM)
    dma = pltpu.SemaphoreType.DMA
    f32 = jnp.float32
    return pl.pallas_call(
        functools.partial(grads_kernel, seq_count, tp_count),
        out_shape=(
            jax.ShapeDtypeStruct((rows, width), f32),
            jax.ShapeDtypeStruct((seq_count, extra, width), f32),
        ),
        in_specs=[vmem, vmem],
        out_specs=(vmem, vmem),
        scratch_shapes=[
            pltpu.VMEM((seq_count, tp_count, rows, width), feat.dtype),
            pltpu.VMEM((seq_count, extra, width), f32),
            pltpu.VMEM((tp_count, rows, width), f32),
            pltpu.VMEM((extra, width), f32),
            pltpu.VMEM((tp_count, rows, width), f32),
            pltpu.VMEM((tp_count, extra, width), f32),
            pltpu.VMEM((seq_count, extra, width), f32),
            dma((2, seq_count)),
            dma((2, seq_count)),
            dma((2, tp_count)),
            dma((2, tp_count)),
            dma((1, seq_count)),
            dma((1, seq_count)),
        ],
        compiler_params=pltpu.CompilerParams(
            collective_id=2, has_side_effects=True, vmem_limit_bytes=32 * 1024 * 1024
        ),
    )(feat, small)


def shards(
    hidden,
    norm_gain,
    query_weight,
    key_weight,
    value_weight,
    output_weight,
    final_gain,
    reward_weight,
    token_ids,
    index_samples,
    feat_weight,
    index_weight,
    first_bias,
    middle_weight,
    second_bias,
    head_weight,
    pair_ids,
):
    precise = lax.Precision.HIGH
    tp_count = lax.axis_size("tensor")
    seq_count = lax.axis_size("seq")
    tp_index = lax.axis_index("tensor")
    seq_index = lax.axis_index("seq")
    tok_seq, part_width = hidden.shape
    width = part_width * tp_count
    local_resp = tok_seq // RESP_LEN
    tok_epi = tok_seq // tp_count

    half_dim = HEAD_DIM // 2
    positions = jnp.arange(RESP_LEN, dtype=jnp.int32)
    freqs = rope_base ** (-(jnp.arange(half_dim, dtype=jnp.float32) * 2.0) / HEAD_DIM)
    angles = positions.astype(jnp.float32)[:, None] * freqs[None, :]
    cosine = jnp.cos(angles)
    sine = jnp.sin(angles)

    share = RESP_LEN // tp_count
    group = tp_count // local_resp
    there = [
        [(t, ((t + p) % local_resp) * group + t // local_resp) for t in range(tp_count)]
        for p in range(local_resp)
    ]
    back = [[(d, t) for t, d in pairs] for pairs in there]

    def piece_of(p):
        return lax.rem(tp_index + p, local_resp)

    def slot_of(p):
        return lax.rem(tp_index // group - p + local_resp, local_resp)

    valid_here = (token_ids != 0).astype(jnp.float32)
    sample_count, index_dim, _ = index_samples.shape
    lanes = jnp.concatenate(
        [index_samples.reshape(sample_count * index_dim, tok_epi), valid_here[None, :]], axis=0
    )
    lanes = jnp.swapaxes(lanes.reshape(lanes.shape[0], local_resp, share), 0, 1)
    moved = jnp.zeros_like(lanes)
    for p in range(local_resp):
        sent = lax.dynamic_index_in_dim(lanes, slot_of(p), 0, keepdims=False)
        got = lax.ppermute(sent, "tensor", back[p])
        moved = lax.dynamic_update_index_in_dim(moved, got, piece_of(p), 0)
    rows_n = sample_count * tok_epi
    z = (
        moved[:, : sample_count * index_dim]
        .reshape(local_resp, sample_count, index_dim, share)
        .transpose(1, 0, 3, 2)
        .reshape(rows_n, index_dim)
    )
    valid = moved[:, sample_count * index_dim]

    gain_parts = norm_gain.reshape(tp_count, part_width)
    pieces = []
    for r in range(local_resp):
        x = lax.all_gather(hidden[r * RESP_LEN : (r + 1) * RESP_LEN], "tensor", axis=0)
        attended = attend(
            x, gain_parts, query_weight, key_weight, value_weight, cosine, sine
        )
        partial = jnp.dot(attended, output_weight, preferred_element_type=jnp.float32).astype(
            jnp.bfloat16
        )
        mixed = lax.psum_scatter(partial, "tensor", scatter_dimension=0, tiled=True)
        own = lax.dynamic_slice_in_dim(x, tp_index * share, share, 1)
        residual = jnp.swapaxes(own, 0, 1).reshape(share, width).astype(jnp.float32)
        summed = residual + mixed.astype(jnp.float32)
        mean_square = jnp.mean(summed * summed, axis=-1, keepdims=True)
        pieces.append(
            (summed * lax.rsqrt(mean_square + norm_eps) * (1.0 + final_gain)).astype(jnp.bfloat16)
        )
    held = jnp.stack(pieces, axis=0)
    features = jnp.zeros_like(held)
    for p in range(local_resp):
        sent = lax.dynamic_index_in_dim(held, piece_of(p), 0, keepdims=False)
        got = lax.ppermute(sent, "tensor", there[p])
        features = lax.dynamic_update_index_in_dim(features, got, slot_of(p), 0)
    features = features.reshape(tok_epi, width)

    feat32 = held.reshape(tok_epi, width).astype(jnp.float32)
    hidden_units = middle_weight.shape[0]
    base = jnp.sum(feat32 * reward_weight, axis=1)
    feat_part = jnp.dot(feat32, feat_weight, precision=precise)
    index_part = jnp.dot(z, index_weight, precision=precise) + first_bias
    first_pre = (index_part.reshape(sample_count, tok_epi, hidden_units) + feat_part).reshape(
        rows_n, hidden_units
    )
    first_act = gelu_tanh(first_pre)
    second_pre = jnp.dot(first_act, middle_weight, precision=precise) + second_bias
    second_act = gelu_tanh(second_pre)
    head_rows = jnp.dot(z, head_weight.T, precision=precise)
    epinet_out = jnp.sum(second_act * head_rows, axis=1).reshape(
        sample_count, local_resp, share
    )
    resp_total = 2 * pair_ids.shape[0]
    owner = seq_index * local_resp + jnp.arange(local_resp, dtype=jnp.int32)
    slot_ids = jnp.arange(resp_total, dtype=jnp.int32)
    owner_table = (owner[:, None] == slot_ids[None, :]).astype(jnp.float32)
    own_totals = jnp.sum(
        (base.reshape(local_resp, share)[None] + epinet_out) * valid[None], axis=2
    )
    own_counts = jnp.zeros((8, local_resp), jnp.float32) + jnp.sum(valid, axis=1)
    part = jnp.concatenate([own_totals, own_counts], axis=0)
    part = jnp.sum(part[:, :, None] * owner_table[None], axis=1)
    part = jnp.pad(part, ((0, 0), (0, 128 - resp_total)))
    sums = sum_everywhere(part, seq_count, tp_count)
    totals = sums[:sample_count, :resp_total]
    counts = sums[sample_count, :resp_total]
    means = totals / counts[None, :]
    sign_table = (pair_ids[:, 0:1] == slot_ids[None, :]).astype(jnp.float32) - (
        pair_ids[:, 1:2] == slot_ids[None, :]
    ).astype(jnp.float32)
    margin = jnp.dot(means, sign_table.T, precision=lax.Precision.HIGHEST)
    pair_margin = margin.T
    margin_grad = -jax.nn.sigmoid(-margin)
    mean_grad = jnp.dot(margin_grad, sign_table, precision=lax.Precision.HIGHEST) / counts[None, :]
    own_grad = jnp.sum(mean_grad[:, None, :] * owner_table[None], axis=2)
    scale = (own_grad[:, :, None] * valid[None]).reshape(rows_n, 1)
    rows_dims = (((0,), (0,)), ((), ()))
    grad_head = lax.dot_general(z * scale, second_act, rows_dims, precision=precise)
    second_grad = scale * head_rows * gelu_slope(second_pre)
    grad_second = jnp.sum(second_grad, axis=0)
    grad_middle = lax.dot_general(first_act, second_grad, rows_dims, precision=precise)
    first_grad = jnp.dot(second_grad, middle_weight.T, precision=precise) * gelu_slope(first_pre)
    grad_first = jnp.sum(first_grad, axis=0)
    grad_index = lax.dot_general(z, first_grad, rows_dims, precision=precise)
    feat_grad = jnp.sum(first_grad.reshape(sample_count, tok_epi, hidden_units), axis=0)
    grad_feature = lax.dot_general(feat32, feat_grad, rows_dims, precision=precise)

    small = jnp.concatenate(
        [grad_middle, grad_index, grad_head, grad_first[None, :], grad_second[None, :]], axis=0
    )
    used = small.shape[0]
    unit = 8 * seq_count
    padded = (used + unit - 1) // unit * unit
    small = jnp.pad(small, ((0, padded - used), (0, 0)))
    small = small.reshape(seq_count, padded // seq_count, hidden_units)
    feat_blocks = grad_feature.astype(jnp.bfloat16).reshape(
        seq_count, tp_count, width // (seq_count * tp_count), hidden_units
    )
    grad_feature, small = reduce_grads(feat_blocks, small, seq_count, tp_count)
    small = small.reshape(padded, hidden_units)
    at = hidden_units
    return (
        features,
        pair_margin,
        grad_feature,
        small[at : at + index_dim],
        small[at + 2 * index_dim],
        small[:at],
        small[at + 2 * index_dim + 1],
        small[at + index_dim : at + 2 * index_dim].T,
    )


def solution(mesh):
    return jax.shard_map(
        shards,
        mesh=mesh,
        in_specs=(
            P("seq", "tensor"),
            P(),
            P(None, "tensor"),
            P(None, "tensor"),
            P(None, "tensor"),
            P("tensor", None),
            P(),
            P(),
            P(("seq", "tensor")),
            P(None, None, ("seq", "tensor")),
            P(),
            P(),
            P(),
            P(),
            P(),
            P(),
            P(),
        ),
        out_specs=(
            P(("seq", "tensor"), None),
            P(),
            P(("seq", "tensor"), None),
            P(),
            P(),
            P(),
            P(),
            P(),
        ),
        check_vma=False,
    )
```
